512 devices in a mesh: occ: 4 (over y), vir: 128 (over x, z, core).
Axes of the slice: x: 4, y: 4, z: 16, core: 2. Of those that a mesh axis runs over, the one named last changes fastest.
Arguments:
- amps: bfloat16 [32, 1024, 128], P('occ', 'vir'), may hold values from -6 to 6
- fitted: bfloat16 [256, 4, 8, 128, 128], P('vir', 'occ'), may hold values from -0.09375 to 0.09375
Outputs:
- resid: float32 [32, 1024, 128], P('occ', 'vir')
The draws below stay inside these ranges and needn't reach their ends.
All inputs are finite; a program needn't handle non-finite values.
Results may differ from the reference program's by a relative error of at most 0.0029.
Values may be sent and summed in bfloat16 or wider, within the bound.
A program may use at most 64 MiB of HBM per device.

```python
import jax
import jax.numpy as jnp
from jax import lax

V = 1024
NQ = 1024
NIRR = 8
PAIRS = 32
BLK = 128
QI = 256
N_OCC = 4


def block_scale(rng, extent, split, smallest, top_value):
    loudness, own = 1.0, jax.random.fold_in(rng, 6)
    for axis_at, blocks in split:
        heights = jnp.exp(jax.random.uniform(jax.random.fold_in(own, axis_at), (blocks,), jnp.float32, smallest / len(split), top_value / len(split)))
        loudness = loudness * jnp.repeat(heights, extent[axis_at] // blocks).reshape([-1 if axis == axis_at else 1 for axis in range(len(extent))])
    return loudness


def normal_values(stream_key, extent, width, bound, shards=(), held_as=jnp.bfloat16):
    level = block_scale(stream_key, extent, shards, -0.22, 0.18) if shards else 1.0
    result = jax.random.normal(stream_key, extent, jnp.float32) * width * level
    return jnp.minimum(jnp.maximum(result, -bound), bound).astype(held_as)


def setup_inputs(seed: int = 0) -> dict:
    seeds = jax.random.split(jax.random.key(seed), 3)
    amps = normal_values(seeds[0], (PAIRS, V, BLK), 1.0, 6.0, ((0, 4), (1, 128)))
    fitted = normal_values(seeds[1], (QI, N_OCC, NIRR, BLK, BLK), 4096 ** -0.5, 0.09375, ((0, 128), (1, 4)))
    return {"amps": amps, "fitted": fitted}


def reference(amps, fitted):
    per_irrep = NQ // (N_OCC * NIRR)
    amp_blocks = amps.reshape(PAIRS, NIRR, BLK, BLK)

    def irrep_block(irrep):
        start_row = (irrep * per_irrep).astype(jnp.int32)
        fitted_block = lax.dynamic_slice_in_dim(fitted, start_row, per_irrep, 0)
        fitted_block = fitted_block.reshape(per_irrep * N_OCC, NIRR, BLK, BLK).astype(jnp.float32)

        def pair_block(amp_block):
            transformed = jnp.einsum("hcd,qhbd->qhcb", amp_block.astype(jnp.float32), fitted_block,
                                     precision=lax.Precision.HIGHEST)
            rounded = lax.optimization_barrier(transformed.astype(jnp.bfloat16))
            transformed = rounded.astype(jnp.float32)
            return jnp.einsum("qhac,qhcb->ab", fitted_block, transformed, precision=lax.Precision.HIGHEST)

        return lax.map(pair_block, amp_blocks)

    stacked = lax.map(irrep_block, jnp.arange(NIRR, dtype=jnp.int32))
    return jnp.transpose(stacked, (1, 0, 2, 3)).reshape(PAIRS, V, BLK)
```

```python
import functools

import jax
import jax.numpy as jnp
from jax import lax
from jax.experimental import pallas as pl
from jax.experimental.pallas import tpu as pltpu
from jax.sharding import PartitionSpec as P

MESH = pl.DeviceIdType.MESH
BF, F32 = jnp.bfloat16, jnp.float32
NT = (((1,), (1,)), ((), ()))
NX, NY, NZ = 4, 4, 16
BLK = 128
PC = 4
ROWS = 8
CH = 4


def slot_of(rel):
    return jnp.maximum(jnp.minimum(2 * rel - 1, 2 * NZ - 2 * rel), 0)


def kernel(amps_ref, fit_ref, out_ref, av, gbuf, tbuf, tp, half, gcat, acc, stage, rbuf,
           loc, ssem, zsem, xsem, ysem, csem, rsem):
    y = lax.axis_index("occ")
    v = lax.axis_index("vir")
    c = lax.rem(v, 2)
    z = lax.rem(lax.div(v, 2), NZ)
    x = lax.div(v, 2 * NZ)
    z8 = lax.rem(z, 8)
    zbase = z - z8

    def dev(dy=0, dx=0, dz=0, core=None):
        yy = lax.rem(y + dy + NY, NY)
        xx = lax.rem(x + dx + NX, NX)
        zz = lax.rem(z + dz + NZ, NZ)
        cc = c if core is None else core
        return (yy, (xx * NZ + zz) * 2 + cc)

    other = 1 - c
    sent = []

    def send(src, dst, recv, to):
        copy = pltpu.make_async_remote_copy(
            src_ref=src, dst_ref=dst, send_sem=ssem.at[len(sent)], recv_sem=recv,
            device_id=to, device_id_type=MESH)
        copy.start()
        sent.append(copy)

    def arrived(ref, sem):
        pltpu.make_async_copy(ref, ref, sem).wait()

    la = pltpu.make_async_copy(amps_ref, av, loc.at[0])
    la.start()
    lg = pltpu.make_async_copy(fit_ref, gbuf.at[0, 0], loc.at[1])
    lg.start()

    barrier = pltpu.get_barrier_semaphore()
    met = [dev(core=other)]
    for d in (4, 3, 2, 1):
        for k in (0, 1):
            met += [dev(dz=d, core=k), dev(dz=-d, core=k)]
    met += [dev(dx=1), dev(dx=-1), dev(dx=2), dev(dy=1), dev(dy=-1)]
    for to in met:
        pl.semaphore_signal(barrier, inc=1, device_id=to, device_id_type=MESH)
    la.wait()
    own = pltpu.make_async_copy(av.at[pl.ds(c * 32, 32)], tbuf.at[0, 0, c], loc.at[0])
    own.start()
    lg.wait()
    own.wait()
    pl.semaphore_wait(barrier, len(met))

    for d in (4, 3, 2, 1):
        for k in (0, 1):
            rows = av.at[pl.ds(k * 32, 32)]
            send(rows, tbuf.at[0, 2 * d, c], zsem.at[d], dev(dz=d, core=k))
            send(rows, tbuf.at[0, 2 * d - 1, c], zsem.at[d], dev(dz=-d, core=k))
    send(av.at[pl.ds(other * 32, 32)], tbuf.at[0, 0, c], zsem.at[0], dev(core=other))

    def chunk(yr, cr, k):
        return gbuf.at[yr, cr, k // 2, pl.ds((k % 2) * 4, 4)]

    for k in range(CH):
        up, down = k, (k + CH // 2) % CH
        send(chunk(0, 0, up), chunk(1, 0, up), ysem.at[1, up], dev(dy=1))
        send(chunk(0, 0, down), chunk(3, 0, down), ysem.at[3, down], dev(dy=-1))
    send(gbuf.at[0, 0], gbuf.at[0, 1], csem.at[0], dev(core=other))

    def along_x(lo, n):
        for dx, xr in ((1, 3), (-1, 1), (2, 2)):
            send(tbuf.at[0, pl.ds(lo, n)], tbuf.at[xr, pl.ds(lo, n)], xsem.at[xr], dev(dx=dx))

    arrived(tbuf.at[0, 0, other], zsem.at[0])
    along_x(0, 1)
    for d in (1, 2, 3, 4):
        arrived(tbuf.at[0, pl.ds(2 * d - 1, 2)], zsem.at[d])
        if d == 4:
            for e in (1, 2, 3):
                send(tbuf.at[0, 8], tbuf.at[0, 8 + 2 * e], zsem.at[4 + e], dev(dz=e))
                send(tbuf.at[0, 7], tbuf.at[0, 7 + 2 * e], zsem.at[4 + e], dev(dz=-e))
            send(tbuf.at[0, 8, 0], tbuf.at[0, 15, 0], zsem.at[8], dev(dz=4))
            send(tbuf.at[0, 7, 1], tbuf.at[0, 15, 1], zsem.at[8], dev(dz=-4))
        along_x(2 * d - 1, 2)

    def relay(k):
        a, b = k, (k + CH // 2) % CH
        arrived(chunk(1, 0, a), ysem.at[1, a])
        arrived(chunk(3, 0, b), ysem.at[3, b])
        if k < CH // 2:
            send(chunk(1, 0, a), chunk(2, 0, a), ysem.at[2, a], dev(dy=1))
            send(chunk(3, 0, b), chunk(2, 0, b), ysem.at[2, b], dev(dy=-1))
        send(chunk(1, 0, a), chunk(1, 1, a), csem.at[1], dev(core=other))
        send(chunk(3, 0, b), chunk(3, 1, b), csem.at[3], dev(core=other))

    relay(0)
    for d in (5, 6, 7):
        arrived(tbuf.at[0, pl.ds(2 * d - 1, 2)], zsem.at[d])
        along_x(2 * d - 1, 2)
    arrived(tbuf.at[0, 15], zsem.at[8])
    along_x(15, 1)
    relay(1)

    acc[...] = jnp.zeros_like(acc)

    def place(xr):
        for za in range(NZ):
            slot = slot_of(lax.rem(za - z + NZ, NZ))
            low = tbuf[xr, slot, 0].astype(F32)
            high = tbuf[xr, slot, 1].astype(F32)
            at = (za % 8) * 16
            for p in range(PC):
                both = jnp.concatenate([low[p * 8:p * 8 + 8], high[p * 8:p * 8 + 8]], axis=0)
                tp[xr, za // 8, p * BLK + at:p * BLK + at + 16, :] = both.astype(BF)

    def block(xr, zh, yrs):
        h = 2 * lax.rem(x + xr, NX) + zh
        amp = tp[xr, zh]
        n = 0
        for yr in yrs:
            for cr in (0, 1):
                for i in (0, 1):
                    g = gbuf[yr, cr, i, h]
                    moved = lax.dot_general(amp, g, NT, preferred_element_type=F32).astype(BF)
                    for p in range(PC):
                        half[n * BLK:(n + 1) * BLK, p * BLK:(p + 1) * BLK] = moved[p * BLK:(p + 1) * BLK]
                    gcat[:, n * BLK:(n + 1) * BLK] = g
                    n += 1
        k = n * BLK
        acc[...] += jnp.dot(gcat[:, :k], half[:k], preferred_element_type=F32)

    def blocks(xr, yrs):
        def body(zh, carry):
            block(xr, zh, yrs)
            return carry
        lax.fori_loop(0, 2, body, 0)

    place(0)
    arrived(gbuf.at[0, 1], csem.at[0])
    blocks(0, (0,))
    relay(2)
    relay(3)
    arrived(gbuf.at[1, 1], csem.at[1])
    arrived(gbuf.at[3, 1], csem.at[3])
    blocks(0, (1, 3))
    for xr in (1, 3, 2):
        arrived(tbuf.at[xr], xsem.at[xr])
        place(xr)
        blocks(xr, (0, 1, 3))
    for k in range(CH):
        arrived(chunk(2, 0, k), ysem.at[2, k])
        send(chunk(2, 0, k), chunk(2, 1, k), csem.at[2], dev(core=other))
    arrived(gbuf.at[2, 1], csem.at[2])

    def last(xr, carry):
        blocks(xr, (2,))
        return carry
    lax.fori_loop(0, NX, last, 0)

    for k in range(16):
        rows = [acc[k * ROWS:(k + 1) * ROWS, p * BLK:(p + 1) * BLK] for p in range(PC)]
        stage[k] = jnp.concatenate(rows, axis=0).astype(BF)
    mine = z8 * 2 + c
    far = list(sent)
    for s in range(1, 16):
        k = lax.rem(mine + s, 16)
        send(stage.at[k], rbuf.at[mine], rsem.at[0],
             (y, (x * NZ + zbase) * 2 + k))
    keep = pltpu.make_async_copy(stage.at[mine], rbuf.at[mine], loc.at[0])
    keep.start()
    for copy in far:
        copy.wait_send()
    keep.wait()
    arrived(rbuf.at[pl.ds(0, 15)], rsem.at[0])
    for k in (0, 1):
        total = rbuf[k].astype(F32)
        for s in range(1, 8):
            total += rbuf[2 * s + k].astype(F32)
        out_ref[k * 32:(k + 1) * 32, :] = total
    for copy in sent[len(far):]:
        copy.wait_send()


def per_device(amps, fitted):
    pairs, rows, width = amps.shape
    flat = amps.reshape(pairs * rows, width)
    blocks = fitted[:, 0]
    vmem, dma = pltpu.VMEM, pltpu.SemaphoreType.DMA
    out = pl.pallas_call(
        kernel,
        out_shape=jax.ShapeDtypeStruct((pairs * rows, width), F32),
        in_specs=[pl.BlockSpec(memory_space=pl.ANY)] * 2,
        out_specs=pl.BlockSpec(memory_space=pltpu.VMEM),
        scratch_shapes=[
            vmem((64, BLK), BF),
            vmem((NY, 2, 2, 8, BLK, BLK), BF),
            vmem((NX, NZ, 2, 32, BLK), BF),
            vmem((NX, 2, PC * BLK, BLK), BF),
            vmem((12 * BLK, PC * BLK), BF),
            vmem((BLK, 12 * BLK), BF),
            vmem((BLK, PC * BLK), F32),
            vmem((16, 32, BLK), BF),
            vmem((16, 32, BLK), BF),
            dma((2,)),
            dma((112,)),
            dma((9,)),
            dma((4,)),
            dma((4, CH)),
            dma((4,)),
            dma((1,)),
        ],
        compiler_params=pltpu.CompilerParams(
            collective_id=0, has_side_effects=True, vmem_limit_bytes=48 << 20),
        cost_estimate=pl.CostEstimate(flops=4 << 30, bytes_accessed=1 << 20, transcendentals=0),
    )(flat, blocks)
    return out.reshape(pairs, rows, width)


def solution(mesh):
    return jax.shard_map(
        per_device,
        mesh=mesh,
        in_specs=(P("occ", "vir", None), P("vir", "occ", None, None, None)),
        out_specs=P("occ", "vir", None),
        check_vma=False,
    )
```

```python
import functools

import jax
import jax.numpy as jnp
from jax import lax
from jax.experimental import pallas as pl
from jax.experimental.pallas import tpu as pltpu
from jax.sharding import PartitionSpec as P

MESH = pl.DeviceIdType.MESH
BF, F32 = jnp.bfloat16, jnp.float32
NT = (((1,), (1,)), ((), ()))
NX, NY, NZ = 4, 4, 16
HZ = NZ // 2
BLK = 128
PC = 4
ROWS = 8
LINE = (0, 3, 1, 2)
FIRST = ((0, 0), (0, 1), (1, 0), (3, 0))
SECOND = ((1, 1), (3, 1))
THIRD = ((2, 0), (2, 1))


def kernel(amps_ref, fit_ref, out_ref, av, gbuf, tbuf, tp, half, gcat, acc, stage, rbuf,
           loc, ssem, zsem, xsem, ysem, csem, esem, rsem):
    y = lax.axis_index("occ")
    v = lax.axis_index("vir")
    c = lax.rem(v, 2)
    z = lax.rem(lax.div(v, 2), NZ)
    x = lax.div(v, 2 * NZ)
    z8 = lax.rem(z, HZ)
    zbase = z - z8
    other = 1 - c
    kind = lax.rem(z, 2)
    zpart = z + 1 - 2 * kind
    at_home = lax.div(z, HZ) == kind

    def dev(dy=0, dx=0, dz=0, core=None):
        yy = lax.rem(y + dy + NY, NY)
        xx = lax.rem(x + dx + NX, NX)
        zz = lax.rem(z + dz + NZ, NZ)
        cc = c if core is None else core
        return (yy, (xx * NZ + zz) * 2 + cc)

    sent = []

    def send(src, dst, recv, to, cond=None):
        copy = pltpu.make_async_remote_copy(
            src_ref=src, dst_ref=dst, send_sem=ssem.at[len(sent)], recv_sem=recv,
            device_id=to, device_id_type=MESH)
        if cond is None:
            copy.start()
        else:
            pl.when(cond)(copy.start)
        sent.append((copy, cond))

    def drain(copies):
        for copy, cond in copies:
            if cond is None:
                copy.wait_send()
            else:
                pl.when(cond)(copy.wait_send)

    def arrived(ref, sem, cond=None):
        copy = pltpu.make_async_copy(ref, ref, sem)
        if cond is None:
            copy.wait()
        else:
            pl.when(cond)(copy.wait)

    la = pltpu.make_async_copy(amps_ref, av, loc.at[0])
    la.start()
    lg = pltpu.make_async_copy(fit_ref.at[:, :, kind], gbuf.at[0, 0, 0], loc.at[1])
    lg.start()

    barrier = pltpu.get_barrier_semaphore()
    met = [dev(core=other)]
    for d in (4, 3, 2, 1):
        for k in (0, 1):
            met += [dev(dz=d, core=k), dev(dz=-d, core=k)]
    met += [dev(dx=1), dev(dx=-1), dev(dx=2), dev(dy=1), dev(dy=-1)]
    for to in met:
        pl.semaphore_signal(barrier, inc=1, device_id=to, device_id_type=MESH)
    la.wait()

    @pl.when(at_home)
    def _():
        own = pltpu.make_async_copy(av.at[pl.ds(c * 32, 32)], tbuf.at[0, z8, c], loc.at[0])
        own.start()
        own.wait()

    lg.wait()
    pl.semaphore_wait(barrier, len(met))

    for d in (4, 3, 2, 1):
        goes = at_home if d % 2 == 0 else jnp.logical_not(at_home)
        for k in (0, 1):
            for s in (d, -d):
                send(av.at[pl.ds(k * 32, 32)], tbuf.at[0, z8, c], zsem.at[z8], dev(dz=s, core=k), goes)
    send(av.at[pl.ds(other * 32, 32)], tbuf.at[0, z8, c], zsem.at[z8], dev(core=other), at_home)

    def swap(k):
        send(fit_ref.at[k, :, 1 - kind], gbuf.at[0, 1, 0, k], esem.at[k], (y, (x * NZ + zpart) * 2 + c))

    def up(zr, k):
        send(gbuf.at[0, zr, 0, k], gbuf.at[1, zr, 0, k], ysem.at[1, zr, k], dev(dy=1))

    def down(zr, k):
        send(gbuf.at[0, zr, 0, k], gbuf.at[3, zr, 0, k], ysem.at[3, zr, k], dev(dy=-1))

    def on_up(zr):
        send(gbuf.at[1, zr, 0, 0], gbuf.at[2, zr, 0, 0], ysem.at[2, zr, 0], dev(dy=1))

    def on_down(zr):
        send(gbuf.at[3, zr, 0, 1], gbuf.at[2, zr, 0, 1], ysem.at[2, zr, 1], dev(dy=-1))

    def across(yr, zr, k):
        send(gbuf.at[yr, zr, 0, k], gbuf.at[yr, zr, 1, k], csem.at[yr, zr], dev(core=other))

    def came(yr, zr, k):
        arrived(gbuf.at[yr, zr, 0, k], ysem.at[yr, zr, k])
        across(yr, zr, k)

    def swapped(k):
        arrived(gbuf.at[0, 1, 0, k], esem.at[k])
        up(1, k)
        down(1, k)
        across(0, 1, k)

    up(0, 0)
    down(0, 1)
    swap(0)

    def source(rel):
        there = lax.rem(z + rel + NZ, NZ)
        return lax.rem(there, HZ), lax.div(there, HZ) == kind

    def along_x(s, slots, cond):
        for slot, dx in slots:
            send(tbuf.at[0, s], tbuf.at[slot, s], xsem.at[slot], dev(dx=dx), cond)

    near, far = ((1, 1), (2, -1)), ((3, 2),)

    def take(rel):
        s, comes = source(rel)
        if rel == 0:
            arrived(tbuf.at[0, s, other], zsem.at[s], comes)
        else:
            arrived(tbuf.at[0, s], zsem.at[s], comes)
        if abs(rel) in (3, 4):
            way = 1 if rel < 0 else -1
            send(tbuf.at[0, s], tbuf.at[0, s], zsem.at[s], dev(dz=2 * way), comes)
            if abs(rel) == 3:
                send(tbuf.at[0, s], tbuf.at[0, s], zsem.at[s], dev(dz=4 * way), comes)
            else:
                k = 0 if rel < 0 else 1
                send(tbuf.at[0, s, k], tbuf.at[0, s, k], zsem.at[s], dev(dz=4 * way), comes)
        along_x(s, near, comes)

    for rel in (0, 1, -1, 2, -2):
        take(rel)
    up(0, 1)
    down(0, 0)
    swap(1)
    for rel in (3, -3, 4, -4):
        take(rel)
    across(0, 0, 0)
    across(0, 0, 1)
    close = (0, 1, -1, 2, -2, 3, -3, 4, -4)
    for rel in close:
        s, comes = source(rel)
        along_x(s, far, comes)
    came(1, 0, 0)
    came(3, 0, 1)
    swapped(0)
    came(1, 0, 1)
    came(3, 0, 0)
    swapped(1)
    distant = (5, -5, 6, -6, 7, -7, 8)
    for rel in distant:
        take(rel)
    on_up(0)
    on_down(0)
    for rel in distant:
        s, comes = source(rel)
        along_x(s, far, comes)

    acc[...] = jnp.zeros_like(acc)

    def place(slot):
        for s in range(HZ):
            low = tbuf[slot, s, 0].astype(F32)
            high = tbuf[slot, s, 1].astype(F32)
            for p in range(PC):
                both = jnp.concatenate([low[p * 8:p * 8 + 8], high[p * 8:p * 8 + 8]], axis=0)
                tp[slot, p * BLK + s * 16:p * BLK + s * 16 + 16, :] = both.astype(BF)

    def block(slot, parts):
        line = lax.rem(x + LINE[slot], NX)
        amp = tp[slot]
        n = 0
        for yr, zr in parts:
            for cr in (0, 1):
                for i in (0, 1):
                    g = gbuf[yr, zr, cr, i, line]
                    moved = lax.dot_general(amp, g, NT, preferred_element_type=F32).astype(BF)
                    for p in range(PC):
                        half[n * BLK:(n + 1) * BLK, p * BLK:(p + 1) * BLK] = moved[p * BLK:(p + 1) * BLK]
                    gcat[:, n * BLK:(n + 1) * BLK] = g
                    n += 1
        k = n * BLK
        acc[...] += jnp.dot(gcat[:, :k], half[:k], preferred_element_type=F32)

    def here(parts):
        for yr, zr in parts:
            arrived(gbuf.at[yr, zr, 1], csem.at[yr, zr])

    place(0)
    here(FIRST)
    block(0, FIRST)
    came(1, 1, 0)
    came(3, 1, 1)
    on_up(1)
    on_down(1)
    came(1, 1, 1)
    came(3, 1, 0)
    for slot in (1, 2):
        arrived(tbuf.at[slot], xsem.at[slot])
        place(slot)
        block(slot, FIRST)
    came(2, 0, 0)
    came(2, 0, 1)
    arrived(tbuf.at[3], xsem.at[3])
    place(3)
    block(3, FIRST)
    here(SECOND)
    block(0, SECOND)
    block(1, SECOND)
    came(2, 1, 0)
    came(2, 1, 1)
    block(2, SECOND)
    block(3, SECOND)
    here(THIRD)
    for slot in range(4):
        block(slot, THIRD)

    for k in range(16):
        rows = [acc[k * ROWS:(k + 1) * ROWS, p * BLK:(p + 1) * BLK] for p in range(PC)]
        stage[k] = jnp.concatenate(rows, axis=0).astype(BF)
    mine = z8 * 2 + c
    before = len(sent)
    for s in range(1, 16):
        k = lax.rem(mine + s, 16)
        send(stage.at[k], rbuf.at[mine], rsem.at[0], (y, (x * NZ + zbase) * 2 + k))
    keep = pltpu.make_async_copy(stage.at[mine], rbuf.at[mine], loc.at[0])
    keep.start()
    drain(sent[:before])
    keep.wait()
    arrived(rbuf.at[pl.ds(0, 15)], rsem.at[0])
    for k in (0, 1):
        total = rbuf[k].astype(F32)
        for s in range(1, HZ):
            total += rbuf[2 * s + k].astype(F32)
        out_ref[k * 32:(k + 1) * 32, :] = total
    drain(sent[before:])


def per_device(amps, fitted):
    pairs, rows, width = amps.shape
    flat = amps.reshape(pairs * rows, width)
    blocks = fitted.reshape(2, NX, 2, BLK, BLK)
    vmem, dma = pltpu.VMEM, pltpu.SemaphoreType.DMA
    out = pl.pallas_call(
        kernel,
        out_shape=jax.ShapeDtypeStruct((pairs * rows, width), F32),
        in_specs=[pl.BlockSpec(memory_space=pl.ANY)] * 2,
        out_specs=pl.BlockSpec(memory_space=pltpu.VMEM),
        scratch_shapes=[
            vmem((64, BLK), BF),
            vmem((NY, 2, 2, 2, NX, BLK, BLK), BF),
            vmem((NX, HZ, 2, 32, BLK), BF),
            vmem((NX, PC * BLK, BLK), BF),
            vmem((16 * BLK, PC * BLK), BF),
            vmem((BLK, 16 * BLK), BF),
            vmem((BLK, PC * BLK), F32),
            vmem((16, 32, BLK), BF),
            vmem((16, 32, BLK), BF),
            dma((2,)),
            dma((136,)),
            dma((HZ,)),
            dma((NX,)),
            dma((NY, 2, 2)),
            dma((NY, 2)),
            dma((2,)),
            dma((1,)),
        ],
        compiler_params=pltpu.CompilerParams(
            collective_id=0, has_side_effects=True, vmem_limit_bytes=60 << 20),
        cost_estimate=pl.CostEstimate(flops=4 << 30, bytes_accessed=1 << 20, transcendentals=0),
    )(flat, blocks)
    return out.reshape(pairs, rows, width)


def solution(mesh):
    return jax.shard_map(
        per_device,
        mesh=mesh,
        in_specs=(P("occ", "vir", None), P("vir", "occ", None, None, None)),
        out_specs=P("occ", "vir", None),
        check_vma=False,
    )
```

```python
import functools

import jax
import jax.numpy as jnp
from jax import lax
from jax.experimental import pallas as pl
from jax.experimental.pallas import tpu as pltpu
from jax.sharding import PartitionSpec as P

MESH = pl.DeviceIdType.MESH
BF, F32 = jnp.bfloat16, jnp.float32
NT = (((1,), (1,)), ((), ()))
NX, NY, NZ = 4, 4, 16
HZ = NZ // 2
BLK = 128
PC = 4
ROWS = 8
LINE = (0, 3, 1, 2)
FIRST = ((0, 0), (0, 1), (1, 0), (3, 0))
SECOND = ((1, 1), (3, 1))
MINE, THEIRS = 0, 1


def kernel(amps_ref, fit_ref, out_ref, av, gbuf, tbuf, tp, half, gcat, acc, handed, stage, rbuf,
           loc, ssem, zsem, xsem, ysem, csem, esem, tsem, hsem, rsem):
    y = lax.axis_index("occ")
    v = lax.axis_index("vir")
    c = lax.rem(v, 2)
    z = lax.rem(lax.div(v, 2), NZ)
    x = lax.div(v, 2 * NZ)
    z8 = lax.rem(z, HZ)
    zbase = z - z8
    other = 1 - c
    kind = lax.rem(z, 2)
    zpart = z + 1 - 2 * kind
    at_home = lax.div(z, HZ) == kind

    def dev(dy=0, dx=0, dz=0, core=None):
        yy = lax.rem(y + dy + NY, NY)
        xx = lax.rem(x + dx + NX, NX)
        zz = lax.rem(z + dz + NZ, NZ)
        cc = c if core is None else core
        return (yy, (xx * NZ + zz) * 2 + cc)

    sent = []

    def send(src, dst, recv, to, cond=None):
        copy = pltpu.make_async_remote_copy(
            src_ref=src, dst_ref=dst, send_sem=ssem.at[len(sent)], recv_sem=recv,
            device_id=to, device_id_type=MESH)
        if cond is None:
            copy.start()
        else:
            pl.when(cond)(copy.start)
        sent.append((copy, cond))

    def drain(copies):
        for copy, cond in copies:
            if cond is None:
                copy.wait_send()
            else:
                pl.when(cond)(copy.wait_send)

    def arrived(ref, sem, cond=None):
        copy = pltpu.make_async_copy(ref, ref, sem)
        if cond is None:
            copy.wait()
        else:
            pl.when(cond)(copy.wait)

    la = pltpu.make_async_copy(amps_ref, av, loc.at[0])
    la.start()
    lg = pltpu.make_async_copy(fit_ref.at[:, :, kind], gbuf.at[0, 0, 0], loc.at[1])
    lg.start()

    barrier = pltpu.get_barrier_semaphore()
    met = [dev(core=other)]
    for d in (4, 3, 2, 1):
        for k in (0, 1):
            met += [dev(dz=d, core=k), dev(dz=-d, core=k)]
    met += [dev(dx=1), dev(dx=-1), dev(dx=2), dev(dy=1), dev(dy=-1)]
    for to in met:
        pl.semaphore_signal(barrier, inc=1, device_id=to, device_id_type=MESH)
    la.wait()

    @pl.when(at_home)
    def _():
        own = pltpu.make_async_copy(av.at[pl.ds(c * 32, 32)], tbuf.at[0, MINE, z8, c], loc.at[0])
        own.start()
        own.wait()

    lg.wait()
    pl.semaphore_wait(barrier, len(met))

    for d in (4, 3, 2, 1):
        goes = at_home if d % 2 == 0 else jnp.logical_not(at_home)
        for k in (0, 1):
            for s in (d, -d):
                send(av.at[pl.ds(k * 32, 32)], tbuf.at[0, MINE, z8, c], zsem.at[z8], dev(dz=s, core=k), goes)
    send(av.at[pl.ds(other * 32, 32)], tbuf.at[0, MINE, z8, c], zsem.at[z8], dev(core=other), at_home)

    def swap(k):
        send(fit_ref.at[k, :, 1 - kind], gbuf.at[0, 1, 0, k], esem.at[k], (y, (x * NZ + zpart) * 2 + c))

    def up(zr, k):
        send(gbuf.at[0, zr, 0, k], gbuf.at[1, zr, 0, k], ysem.at[1, zr, k], dev(dy=1))

    def down(zr, k):
        send(gbuf.at[0, zr, 0, k], gbuf.at[3, zr, 0, k], ysem.at[3, zr, k], dev(dy=-1))

    def on_up(zr):
        send(gbuf.at[1, zr, 0, 0], gbuf.at[2, zr, 0, 0], ysem.at[2, zr, 0], dev(dy=1))

    def on_down(zr):
        send(gbuf.at[3, zr, 0, 1], gbuf.at[2, zr, 0, 1], ysem.at[2, zr, 1], dev(dy=-1))

    def across(yr, zr, k):
        send(gbuf.at[yr, zr, 0, k], gbuf.at[yr, zr, 1, k], csem.at[yr, zr], dev(core=other))

    def came(yr, zr, k):
        arrived(gbuf.at[yr, zr, 0, k], ysem.at[yr, zr, k])
        across(yr, zr, k)

    def swapped(k):
        arrived(gbuf.at[0, 1, 0, k], esem.at[k])
        up(1, k)
        down(1, k)
        across(0, 1, k)

    up(0, 0)
    down(0, 1)
    swap(0)
    up(0, 1)
    down(0, 0)
    swap(1)

    def source(rel):
        there = lax.rem(z + rel + NZ, NZ)
        return lax.rem(there, HZ), lax.div(there, HZ) == kind

    def along_x(s, slots, cond):
        for slot, dx in slots:
            send(tbuf.at[0, MINE, s], tbuf.at[slot, MINE, s], xsem.at[slot], dev(dx=dx), cond)

    near, far = ((1, 1), (2, -1)), ((3, 2),)

    def take(rel):
        s, comes = source(rel)
        if rel == 0:
            arrived(tbuf.at[0, MINE, s, other], zsem.at[s], comes)
        else:
            arrived(tbuf.at[0, MINE, s], zsem.at[s], comes)
        if abs(rel) in (3, 4):
            way = 1 if rel < 0 else -1
            send(tbuf.at[0, MINE, s], tbuf.at[0, MINE, s], zsem.at[s], dev(dz=2 * way), comes)
            if abs(rel) == 3:
                send(tbuf.at[0, MINE, s], tbuf.at[0, MINE, s], zsem.at[s], dev(dz=4 * way), comes)
            else:
                k = 0 if rel < 0 else 1
                send(tbuf.at[0, MINE, s, k], tbuf.at[0, MINE, s, k], zsem.at[s], dev(dz=4 * way), comes)
        along_x(s, near, comes)

    for rel in (0, 1, -1, 2, -2):
        take(rel)
    for rel in (3, -3, 4, -4):
        take(rel)
    across(0, 0, 0)
    across(0, 0, 1)
    close = (0, 1, -1, 2, -2, 3, -3, 4, -4)
    for rel in close:
        s, comes = source(rel)
        along_x(s, far, comes)
    came(1, 0, 0)
    came(3, 0, 1)
    swapped(0)
    came(1, 0, 1)
    came(3, 0, 0)
    swapped(1)
    distant = (5, -5, 6, -6, 7, -7, 8)
    for rel in distant:
        take(rel)
    on_up(0)
    on_down(0)
    for rel in distant:
        s, comes = source(rel)
        along_x(s, far, comes)

    acc[...] = jnp.zeros_like(acc)

    def share(slot):
        send(tbuf.at[slot, MINE], tbuf.at[slot, THEIRS], tsem.at[slot], dev(core=other))

    def place(slot, who):
        for s in range(HZ):
            low = tbuf[slot, who, s, 0].astype(F32)
            high = tbuf[slot, who, s, 1].astype(F32)
            for p in range(PC):
                both = jnp.concatenate([low[p * 8:p * 8 + 8], high[p * 8:p * 8 + 8]], axis=0)
                tp[slot, who, p * BLK + s * 16:p * BLK + s * 16 + 16, :] = both.astype(BF)

    def block(slots, who, parts, cores=(0, 1)):
        n = 0
        for slot in slots:
            line = lax.rem(x + LINE[slot], NX)
            amp = tp[slot, who]
            for yr, zr in parts:
                for cr in cores:
                    for i in (0, 1):
                        g = gbuf[yr, zr, cr, i, line]
                        moved = lax.dot_general(amp, g, NT, preferred_element_type=F32).astype(BF)
                        for p in range(PC):
                            half[n * BLK:(n + 1) * BLK, p * BLK:(p + 1) * BLK] = moved[p * BLK:(p + 1) * BLK]
                        gcat[:, n * BLK:(n + 1) * BLK] = g
                        n += 1
        k = n * BLK
        acc[who] += jnp.dot(gcat[:, :k], half[:k], preferred_element_type=F32)

    def here(parts):
        for yr, zr in parts:
            arrived(gbuf.at[yr, zr, 1], csem.at[yr, zr])

    share(0)
    place(0, MINE)
    here(FIRST)
    block((0,), MINE, FIRST)
    came(1, 1, 0)
    came(3, 1, 1)
    on_up(1)
    on_down(1)
    came(1, 1, 1)
    came(3, 1, 0)
    for slot in (1, 2):
        arrived(tbuf.at[slot, MINE], xsem.at[slot])
        share(slot)
        place(slot, MINE)
        block((slot,), MINE, FIRST)
    arrived(tbuf.at[3, MINE], xsem.at[3])
    share(3)
    place(3, MINE)
    block((3,), MINE, FIRST)
    here(SECOND)
    block((0, 1), MINE, SECOND)
    block((2, 3), MINE, SECOND)
    for slot in range(4):
        arrived(tbuf.at[slot, THEIRS], tsem.at[slot])
        place(slot, THEIRS)
    for zr in (0, 1):
        for k in (0, 1):
            arrived(gbuf.at[2, zr, 0, k], ysem.at[2, zr, k])
        block((0, 1, 2, 3), THEIRS, ((2, zr),), (0,))
        if zr == 1:
            send(acc.at[THEIRS], handed, hsem.at[0], dev(core=other))
        block((0, 1, 2, 3), MINE, ((2, zr),), (0,))
    arrived(handed, hsem.at[0])
    acc[MINE] += handed[...]

    for k in range(16):
        rows = [acc[MINE, k * ROWS:(k + 1) * ROWS, p * BLK:(p + 1) * BLK] for p in range(PC)]
        stage[k] = jnp.concatenate(rows, axis=0).astype(BF)
    mine = z8 * 2 + c
    before = len(sent)
    for s in range(1, 16):
        k = lax.rem(mine + s, 16)
        send(stage.at[k], rbuf.at[mine], rsem.at[0], (y, (x * NZ + zbase) * 2 + k))
    keep = pltpu.make_async_copy(stage.at[mine], rbuf.at[mine], loc.at[0])
    keep.start()
    drain(sent[:before])
    keep.wait()
    arrived(rbuf.at[pl.ds(0, 15)], rsem.at[0])
    for k in (0, 1):
        total = rbuf[k].astype(F32)
        for s in range(1, HZ):
            total += rbuf[2 * s + k].astype(F32)
        out_ref[k * 32:(k + 1) * 32, :] = total
    drain(sent[before:])


def per_device(amps, fitted):
    pairs, rows, width = amps.shape
    flat = amps.reshape(pairs * rows, width)
    blocks = fitted.reshape(2, NX, 2, BLK, BLK)
    vmem, dma = pltpu.VMEM, pltpu.SemaphoreType.DMA
    out = pl.pallas_call(
        kernel,
        out_shape=jax.ShapeDtypeStruct((pairs * rows, width), F32),
        in_specs=[pl.BlockSpec(memory_space=pl.ANY)] * 2,
        out_specs=pl.BlockSpec(memory_space=pltpu.VMEM),
        scratch_shapes=[
            vmem((64, BLK), BF),
            vmem((NY, 2, 2, 2, NX, BLK, BLK), BF),
            vmem((NX, 2, HZ, 2, 32, BLK), BF),
            vmem((NX, 2, PC * BLK, BLK), BF),
            vmem((16 * BLK, PC * BLK), BF),
            vmem((BLK, 16 * BLK), BF),
            vmem((2, BLK, PC * BLK), F32),
            vmem((BLK, PC * BLK), F32),
            vmem((16, 32, BLK), BF),
            vmem((16, 32, BLK), BF),
            dma((2,)),
            dma((136,)),
            dma((HZ,)),
            dma((NX,)),
            dma((NY, 2, 2)),
            dma((NY, 2)),
            dma((2,)),
            dma((NX,)),
            dma((1,)),
            dma((1,)),
        ],
        compiler_params=pltpu.CompilerParams(
            collective_id=0, has_side_effects=True, vmem_limit_bytes=60 << 20),
        cost_estimate=pl.CostEstimate(flops=4 << 30, bytes_accessed=1 << 20, transcendentals=0),
    )(flat, blocks)
    return out.reshape(pairs, rows, width)


def solution(mesh):
    return jax.shard_map(
        per_device,
        mesh=mesh,
        in_specs=(P("occ", "vir", None), P("vir", "occ", None, None, None)),
        out_specs=P("occ", "vir", None),
        check_vma=False,
    )
```

```python
import functools

import jax
import jax.numpy as jnp
from jax import lax
from jax.experimental import pallas as pl
from jax.experimental.pallas import tpu as pltpu
from jax.sharding import PartitionSpec as P

MESH = pl.DeviceIdType.MESH
BF, F32 = jnp.bfloat16, jnp.float32
NT = (((1,), (1,)), ((), ()))
NX, NY, NZ = 4, 4, 16
HZ = NZ // 2
BLK = 128
PC = 4
ROWS = 8
LINE = (0, 3, 1, 2)
FIRST = ((0, 0), (0, 1), (1, 0), (3, 0))
SECOND = ((1, 1), (3, 1))
MINE, THEIRS = 0, 1


def kernel(amps_ref, fit_ref, out_ref, av, gbuf, tbuf, tp, half, gcat, acc, handed, stage, rbuf,
           loc, ssem, zsem, xsem, ysem, csem, esem, tsem, hsem, rsem):
    y = lax.axis_index("occ")
    v = lax.axis_index("vir")
    c = lax.rem(v, 2)
    z = lax.rem(lax.div(v, 2), NZ)
    x = lax.div(v, 2 * NZ)
    z8 = lax.rem(z, HZ)
    zbase = z - z8
    other = 1 - c
    kind = lax.rem(z, 2)
    zpart = z + 1 - 2 * kind
    at_home = lax.div(z, HZ) == kind

    def dev(dy=0, dx=0, dz=0, core=None):
        yy = lax.rem(y + dy + NY, NY)
        xx = lax.rem(x + dx + NX, NX)
        zz = lax.rem(z + dz + NZ, NZ)
        cc = c if core is None else core
        return (yy, (xx * NZ + zz) * 2 + cc)

    sent = []

    def send(src, dst, recv, to, cond=None):
        copy = pltpu.make_async_remote_copy(
            src_ref=src, dst_ref=dst, send_sem=ssem.at[len(sent)], recv_sem=recv,
            device_id=to, device_id_type=MESH)
        if cond is None:
            copy.start()
        else:
            pl.when(cond)(copy.start)
        sent.append((copy, cond))

    def drain(copies):
        for copy, cond in copies:
            if cond is None:
                copy.wait_send()
            else:
                pl.when(cond)(copy.wait_send)

    def arrived(ref, sem, cond=None):
        copy = pltpu.make_async_copy(ref, ref, sem)
        if cond is None:
            copy.wait()
        else:
            pl.when(cond)(copy.wait)

    la = pltpu.make_async_copy(amps_ref, av, loc.at[0])
    la.start()
    lg = pltpu.make_async_copy(fit_ref.at[:, :, kind], gbuf.at[0, 0, 0], loc.at[1])
    lg.start()

    barrier = pltpu.get_barrier_semaphore()
    met = [dev(core=other)]
    for d in (4, 3, 2, 1):
        for k in (0, 1):
            met += [dev(dz=d, core=k), dev(dz=-d, core=k)]
    met += [dev(dx=1), dev(dx=-1), dev(dx=2), dev(dy=1), dev(dy=-1)]
    for to in met:
        pl.semaphore_signal(barrier, inc=1, device_id=to, device_id_type=MESH)
    la.wait()

    @pl.when(at_home)
    def _():
        own = pltpu.make_async_copy(av.at[pl.ds(c * 32, 32)], tbuf.at[0, MINE, z8, c], loc.at[0])
        own.start()
        own.wait()

    lg.wait()
    pl.semaphore_wait(barrier, len(met))

    def swap(k):
        send(fit_ref.at[k, :, 1 - kind], gbuf.at[0, 1, 0, k], esem.at[k], (y, (x * NZ + zpart) * 2 + c))

    def up(zr, k):
        send(gbuf.at[0, zr, 0, k], gbuf.at[1, zr, 0, k], ysem.at[1, zr, k], dev(dy=1))

    def down(zr, k):
        send(gbuf.at[0, zr, 0, k], gbuf.at[3, zr, 0, k], ysem.at[3, zr, k], dev(dy=-1))

    def on_up(zr):
        send(gbuf.at[1, zr, 0, 0], gbuf.at[2, zr, 0, 0], ysem.at[2, zr, 0], dev(dy=1))

    def on_down(zr):
        send(gbuf.at[3, zr, 0, 1], gbuf.at[2, zr, 0, 1], ysem.at[2, zr, 1], dev(dy=-1))

    def across(yr, zr, k):
        send(gbuf.at[yr, zr, 0, k], gbuf.at[yr, zr, 1, k], csem.at[yr, zr], dev(core=other))

    def came(yr, zr, k):
        arrived(gbuf.at[yr, zr, 0, k], ysem.at[yr, zr, k])
        across(yr, zr, k)

    def swapped(k):
        arrived(gbuf.at[0, 1, 0, k], esem.at[k])
        up(1, k)
        down(1, k)
        across(0, 1, k)

    up(0, 0)
    down(0, 1)
    up(0, 1)
    down(0, 0)

    for d in (4, 3, 2, 1):
        goes = at_home if d % 2 == 0 else jnp.logical_not(at_home)
        for k in (0, 1):
            for s in (d, -d):
                send(av.at[pl.ds(k * 32, 32)], tbuf.at[0, MINE, z8, c], zsem.at[z8], dev(dz=s, core=k), goes)
    send(av.at[pl.ds(other * 32, 32)], tbuf.at[0, MINE, z8, c], zsem.at[z8], dev(core=other), at_home)

    swap(0)
    swap(1)

    def source(rel):
        there = lax.rem(z + rel + NZ, NZ)
        return lax.rem(there, HZ), lax.div(there, HZ) == kind

    def along_x(s, slots, cond):
        for slot, dx in slots:
            send(tbuf.at[0, MINE, s], tbuf.at[slot, MINE, s], xsem.at[slot], dev(dx=dx), cond)

    near, far = ((1, 1), (2, -1)), ((3, 2),)

    def take(rel):
        s, comes = source(rel)
        if rel == 0:
            arrived(tbuf.at[0, MINE, s, other], zsem.at[s], comes)
        else:
            arrived(tbuf.at[0, MINE, s], zsem.at[s], comes)
        if abs(rel) in (3, 4):
            way = 1 if rel < 0 else -1
            send(tbuf.at[0, MINE, s], tbuf.at[0, MINE, s], zsem.at[s], dev(dz=2 * way), comes)
            if abs(rel) == 3:
                send(tbuf.at[0, MINE, s], tbuf.at[0, MINE, s], zsem.at[s], dev(dz=4 * way), comes)
            else:
                k = 0 if rel < 0 else 1
                send(tbuf.at[0, MINE, s, k], tbuf.at[0, MINE, s, k], zsem.at[s], dev(dz=4 * way), comes)
        along_x(s, near, comes)

    for rel in (0, 1, -1, 2, -2):
        take(rel)
    for rel in (3, -3, 4, -4):
        take(rel)
    across(0, 0, 0)
    across(0, 0, 1)
    close = (0, 1, -1, 2, -2, 3, -3, 4, -4)
    for rel in close:
        s, comes = source(rel)
        along_x(s, far, comes)
    came(1, 0, 0)
    came(3, 0, 1)
    swapped(0)
    came(1, 0, 1)
    came(3, 0, 0)
    swapped(1)
    distant = (5, -5, 6, -6, 7, -7, 8)
    for rel in distant:
        take(rel)
    on_up(0)
    on_down(0)
    for rel in distant:
        s, comes = source(rel)
        along_x(s, far, comes)

    acc[...] = jnp.zeros_like(acc)

    def share(slot):
        send(tbuf.at[slot, MINE], tbuf.at[slot, THEIRS], tsem.at[slot], dev(core=other))

    def place(slot, who):
        for s in range(HZ):
            low = tbuf[slot, who, s, 0].astype(F32)
            high = tbuf[slot, who, s, 1].astype(F32)
            for p in range(PC):
                both = jnp.concatenate([low[p * 8:p * 8 + 8], high[p * 8:p * 8 + 8]], axis=0)
                tp[slot, who, p * BLK + s * 16:p * BLK + s * 16 + 16, :] = both.astype(BF)

    def block(slots, who, parts, cores=(0, 1)):
        n = 0
        for slot in slots:
            line = lax.rem(x + LINE[slot], NX)
            amp = tp[slot, who]
            for yr, zr in parts:
                for cr in cores:
                    for i in (0, 1):
                        g = gbuf[yr, zr, cr, i, line]
                        moved = lax.dot_general(amp, g, NT, preferred_element_type=F32).astype(BF)
                        for p in range(PC):
                            half[n * BLK:(n + 1) * BLK, p * BLK:(p + 1) * BLK] = moved[p * BLK:(p + 1) * BLK]
                        gcat[:, n * BLK:(n + 1) * BLK] = g
                        n += 1
        k = n * BLK
        acc[who] += jnp.dot(gcat[:, :k], half[:k], preferred_element_type=F32)

    def here(parts):
        for yr, zr in parts:
            arrived(gbuf.at[yr, zr, 1], csem.at[yr, zr])

    share(0)
    place(0, MINE)
    here(FIRST)
    block((0,), MINE, FIRST)
    came(1, 1, 0)
    came(3, 1, 1)
    on_up(1)
    on_down(1)
    came(1, 1, 1)
    came(3, 1, 0)
    for slot in (1, 2):
        arrived(tbuf.at[slot, MINE], xsem.at[slot])
        share(slot)
        place(slot, MINE)
        block((slot,), MINE, FIRST)
    here(SECOND)
    block((0, 1), MINE, SECOND)
    for slot in (0, 1, 2):
        arrived(tbuf.at[slot, THEIRS], tsem.at[slot])
        place(slot, THEIRS)
    arrived(tbuf.at[3, MINE], xsem.at[3])
    share(3)
    place(3, MINE)
    block((3,), MINE, FIRST)
    block((2, 3), MINE, SECOND)
    arrived(tbuf.at[3, THEIRS], tsem.at[3])
    place(3, THEIRS)
    for zr in (0, 1):
        for k in (0, 1):
            arrived(gbuf.at[2, zr, 0, k], ysem.at[2, zr, k])
        block((0, 1, 2, 3), THEIRS, ((2, zr),), (0,))
        if zr == 1:
            send(acc.at[THEIRS], handed, hsem.at[0], dev(core=other))
        block((0, 1, 2, 3), MINE, ((2, zr),), (0,))
    arrived(handed, hsem.at[0])
    acc[MINE] += handed[...]

    for k in range(16):
        rows = [acc[MINE, k * ROWS:(k + 1) * ROWS, p * BLK:(p + 1) * BLK] for p in range(PC)]
        stage[k] = jnp.concatenate(rows, axis=0).astype(BF)
    mine = z8 * 2 + c
    before = len(sent)
    for s in range(1, 16):
        k = lax.rem(mine + s, 16)
        send(stage.at[k], rbuf.at[mine], rsem.at[0], (y, (x * NZ + zbase) * 2 + k))
    keep = pltpu.make_async_copy(stage.at[mine], rbuf.at[mine], loc.at[0])
    keep.start()
    drain(sent[:before])
    keep.wait()
    arrived(rbuf.at[pl.ds(0, 15)], rsem.at[0])
    for k in (0, 1):
        total = rbuf[k].astype(F32)
        for s in range(1, HZ):
            total += rbuf[2 * s + k].astype(F32)
        out_ref[k * 32:(k + 1) * 32, :] = total
    drain(sent[before:])


def per_device(amps, fitted):
    pairs, rows, width = amps.shape
    flat = amps.reshape(pairs * rows, width)
    blocks = fitted.reshape(2, NX, 2, BLK, BLK)
    vmem, dma = pltpu.VMEM, pltpu.SemaphoreType.DMA
    out = pl.pallas_call(
        kernel,
        out_shape=jax.ShapeDtypeStruct((pairs * rows, width), F32),
        in_specs=[pl.BlockSpec(memory_space=pl.ANY)] * 2,
        out_specs=pl.BlockSpec(memory_space=pltpu.VMEM),
        scratch_shapes=[
            vmem((64, BLK), BF),
            vmem((NY, 2, 2, 2, NX, BLK, BLK), BF),
            vmem((NX, 2, HZ, 2, 32, BLK), BF),
            vmem((NX, 2, PC * BLK, BLK), BF),
            vmem((16 * BLK, PC * BLK), BF),
            vmem((BLK, 16 * BLK), BF),
            vmem((2, BLK, PC * BLK), F32),
            vmem((BLK, PC * BLK), F32),
            vmem((16, 32, BLK), BF),
            vmem((16, 32, BLK), BF),
            dma((2,)),
            dma((136,)),
            dma((HZ,)),
            dma((NX,)),
            dma((NY, 2, 2)),
            dma((NY, 2)),
            dma((2,)),
            dma((NX,)),
            dma((1,)),
            dma((1,)),
        ],
        compiler_params=pltpu.CompilerParams(
            collective_id=0, has_side_effects=True, vmem_limit_bytes=60 << 20),
        cost_estimate=pl.CostEstimate(flops=4 << 30, bytes_accessed=1 << 20, transcendentals=0),
    )(flat, blocks)
    return out.reshape(pairs, rows, width)


def solution(mesh):
    return jax.shard_map(
        per_device,
        mesh=mesh,
        in_specs=(P("occ", "vir", None), P("vir", "occ", None, None, None)),
        out_specs=P("occ", "vir", None),
        check_vma=False,
    )
```
